32 devices in a mesh: section: 2 (over x), expert: 16 (over z, y, core).
Axes of the slice: x: 2, y: 2, z: 4, core: 2. Of those that a mesh axis runs over, the one named last changes fastest.
Arguments:
- next_grad: bfloat16 [2, 256, 3584], P('section', 'expert'), may hold values from -6 to 6
- routes: int32 [2, 256, 8], P('section', 'expert'), may hold values from 0 to 15, all different within a row; in each aligned block of 16 rows (0 to 15, 16 to 31, ..., all dimensions but the last counted through in order) at most 16 rows name the same one
- gates: float32 [2, 256, 8], P('section', 'expert'), may hold values from 0.1 to 0.6
- saved: bfloat16 [2, 16, 256, 2048], P('section', 'expert'), may hold values from -5 to 5
- w_down: bfloat16 [16, 1024, 3584], P('expert'), may hold values from -0.1875 to 0.1875
Outputs:
- hidden_grads: bfloat16 [2, 16, 256, 2048], P('section', 'expert')
The draws below stay inside these ranges and needn't reach their ends.
Inputs may be any that keep to these rules, and one draw needn't show every extreme that they name: `routes`: each row names 8 different experts; among the 16 rows of one device no expert is named by more than 16 rows, and in every draw some expert is named by exactly 16 rows of some device.
All inputs are finite; a program needn't handle non-finite values.
Results may differ from the reference program's by a relative error of at most 0.005.
Values may be sent and summed in bfloat16 or wider, within the bound.
No kernel may reach another device: no remote copies, remote signals or barrier semaphores. Data moves between devices by JAX's collectives and lax.ppermute only.
A program may use at most 64 MiB of HBM per device.

```python
import math
import jax
import jax.numpy as jnp
import numpy as np
from jax import lax

D = 3584
H = 1024
TOP = 8
TOK_DEV = 16
EXPERTS = 16
TOKENS = 256
MOST = 16
SLOTS = 256
N_SECTION = 2
N_EXPERT = 16


def levels(own_key, dims, split, smallest, top_value):
    loudness, own = 1.0, jax.random.fold_in(own_key, 6)
    for dim, parts in split:
        heights = jnp.exp(jax.random.uniform(jax.random.fold_in(own, dim), (parts,), jnp.float32, smallest / len(split), top_value / len(split)))
        loudness = loudness * jnp.repeat(heights, dims[dim] // parts).reshape([-1 if axis == dim else 1 for axis in range(len(dims))])
    return loudness


def shared_out(own_key, own, number, rows, count, top, most, slope):
    ranking = jax.random.permutation(own_key, count)
    packed, common = shares(count, rows * top, most, slope, True), shares(count, rows * top, most, slope, False)
    places = jnp.arange(count)

    def named(sizes, rotation):
        used = int((sizes > 0).sum())
        fixed = max(1, used // 4)
        passed = fixed + (places - fixed + rotation * (used - fixed)) % max(1, count - fixed)
        return jnp.zeros((count,), jnp.int32).at[ranking[jnp.where(places < fixed, places, passed)]].set(jnp.asarray(sizes, jnp.int32))

    sizes = jnp.where(number % 4 == 0, named(packed, number // 4), named(common, number - number // 4 - 1))
    mixed = jax.random.permutation(jax.random.fold_in(own, 3), count)
    donor, taker = mixed[0:count // 2 * 2:2], mixed[1:count // 2 * 2:2]
    margin = jnp.minimum(sizes[donor] - 1, most - sizes[taker]) // 2
    margin = jnp.where((donor == ranking[0]) | (taker == ranking[0]) | (sizes[taker] == 0), 0, jnp.maximum(margin, 0))
    passed = jax.random.randint(jax.random.fold_in(own, 4), (count // 2,), 0, 1 << 20) % (margin + 1)
    sizes = sizes.at[donor].add(-passed).at[taker].add(passed)
    members = jnp.searchsorted(jnp.cumsum(sizes), jnp.arange(rows * top), side="right").astype(jnp.int32)
    grid = members.reshape(top, rows).T
    grid = grid[jax.random.permutation(jax.random.fold_in(own, 1), rows)]
    rotation = jax.random.randint(jax.random.fold_in(own, 2), (rows, 1), 0, top)
    return jnp.take_along_axis(grid, (jnp.arange(top)[None, :] + rotation) % top, axis=1)


def shares(count, total, most, skew, full):
    weights = [(1 << 20) // math.isqrt(standing ** skew) + 1 for standing in range(1, count + 1)]
    largest = most if full else min(most, max(-(-total // count), total * weights[0] // sum(weights)))
    least = 1 if total - largest >= count - 1 else 0
    holding, rest = [largest] + [least] * (count - 1), total - largest - least * (count - 1)
    while rest > 0:
        candidates = [i for i in range(1, count) if holding[i] < largest] or [i for i in range(1, count) if holding[i] < most]
        whole, budget = sum([weights[i] for i in candidates]), rest
        for i in candidates:
            extra = min(most - holding[i], max(1, budget * weights[i] // whole), rest)
            holding[i] = holding[i] + extra
            rest = rest - extra
    return np.array(holding)


def normal_values(stream_key, shape, width, bound, cuts=(), kind=jnp.bfloat16):
    result = jax.random.normal(stream_key, shape, jnp.float32) * width
    if len(cuts) > 0:
        result = levels(stream_key, shape, cuts, -0.22, 0.18) * result
    return jnp.clip(result, min=-bound, max=bound).astype(kind)


def setup_inputs(seed: int = 0) -> dict:
    key_list = jax.random.split(jax.random.key(seed), 6)
    next_grad = normal_values(key_list[0], (N_SECTION, TOKENS, D), 1.0, 6.0, ((0, 2), (1, 16)))
    routes_keys = jax.random.split(jax.random.fold_in(key_list[1], 1), N_SECTION * TOKENS // TOK_DEV)
    routes_turns = jax.random.permutation(jax.random.fold_in(key_list[1], 3), N_SECTION * TOKENS // TOK_DEV)
    routes = jax.vmap(lambda own, number: shared_out(jax.random.fold_in(key_list[1], 2), own, number, TOK_DEV, EXPERTS, TOP, MOST, 2))(routes_keys, routes_turns).reshape((N_SECTION, TOKENS, TOP))
    gates = jnp.clip(0.1 + 0.5 * jax.random.uniform(key_list[2], (N_SECTION, TOKENS, TOP), jnp.float32) ** levels(key_list[2], (N_SECTION, TOKENS, TOP), ((0, 2), (1, 16)), -0.2, 0.2), 0.1, 0.6)
    saved = normal_values(key_list[3], (N_SECTION, EXPERTS, SLOTS, 2 * H), 1.0, 5.0, ((0, 2), (1, 16)))
    w_down = normal_values(key_list[4], (EXPERTS, H, D), H ** -0.5, 0.1875, ((0, 16),))
    return {"next_grad": next_grad, "routes": routes, "gates": gates, "saved": saved, "w_down": w_down}


def one_section(args, w_down):
    grad, route, gate, saved_s = args
    expert_ids = jnp.arange(EXPERTS, dtype=jnp.int32)
    hit = jnp.sum((route[:, :, None] == expert_ids[None, None, :]).astype(jnp.int32), axis=1)
    blocks = hit.reshape(N_EXPERT, TOK_DEV, EXPERTS)
    before = (jnp.cumsum(blocks, axis=1) - blocks).reshape(TOKENS, EXPERTS).astype(jnp.int32)
    position = jnp.take_along_axis(before, route, axis=1).astype(jnp.int32)
    source = (jnp.arange(TOKENS, dtype=jnp.int32) // TOK_DEV)[:, None]
    slot = (source * MOST + position).astype(jnp.int32)
    rows = (gate[:, :, None] * grad[:, None, :].astype(jnp.float32)).astype(jnp.bfloat16)
    buffer = jnp.zeros((EXPERTS, SLOTS, D), jnp.bfloat16).at[route, slot].set(rows)

    def per_expert(pair):
        block, mat = pair
        return jnp.dot(block, mat.T, preferred_element_type=jnp.float32)

    hidden = lax.map(per_expert, (buffer, w_down))
    pre_gate = saved_s[..., :H].astype(jnp.float32)
    pre_up = saved_s[..., H:].astype(jnp.float32)
    sig = jax.nn.sigmoid(pre_gate)
    d_up = hidden * pre_gate * sig
    d_gate = hidden * pre_up * sig * (1.0 + pre_gate * (1.0 - sig))
    return jnp.concatenate([d_gate, d_up], axis=-1).astype(jnp.bfloat16)


def reference(next_grad, routes, gates, saved, w_down):
    incoming = jnp.roll(next_grad, -1, axis=0)
    return lax.map(lambda args: one_section(args, w_down), (incoming, routes, gates, saved))
```

```python
import functools

import jax
import jax.numpy as jnp
from jax import lax
from jax.experimental import pallas as pl
from jax.experimental.pallas import tpu as pltpu
from jax.sharding import PartitionSpec as P

CORE = 1
PAIR = 2
ROWS = 16
MIB = 1024 * 1024


def exchange(x, delta):
    peers = lax.axis_size("expert")
    return lax.ppermute(x, "expert", [(i, i ^ delta) for i in range(peers)])


def from_next_section(x, delta):
    sections, peers = lax.axis_size("section"), lax.axis_size("expert")
    pairs = [
        (s * peers + i, (s - 1) % sections * peers + (i ^ delta))
        for s in range(sections)
        for i in range(peers)
    ]
    return lax.ppermute(x, ("section", "expert"), pairs)


def assign_table(routes, gates, experts):
    match = routes[:, :, None] == jnp.arange(experts, dtype=jnp.int32)[None, None, :]
    table = jnp.sum(jnp.where(match, gates[:, :, None], 0.0), axis=1)
    high = lax.reduce_precision(table, exponent_bits=8, mantissa_bits=7)
    low = lax.reduce_precision(table - high, exponent_bits=8, mantissa_bits=7)
    return jnp.concatenate([high, low], axis=1).astype(jnp.bfloat16)


def with_tables(send, chunk, tables, delta):
    width = chunk.shape[1]
    keys = list(tables)
    got = send(jnp.concatenate([chunk] + [tables[k] for k in keys], axis=1))
    each = tables[keys[0]].shape[1]
    rest = {k ^ delta: got[:, width + n * each : width + (n + 1) * each] for n, k in enumerate(keys)}
    return got[:, :width], rest


def gather_tokens(grad, table):
    peers = lax.axis_size("expert")
    top = peers // 2
    far = from_next_section(grad, top)
    near = from_next_section(grad, 0)
    beside = from_next_section(grad, PAIR)
    tables = {0: table, top: exchange(table, top)}
    line = {0: near, top: far}
    delta = top // 2
    while delta > PAIR:
        held = list(line)
        for k in held[:-1]:
            line[k ^ delta] = exchange(line[k], delta)
        last = held[-1]
        line[last ^ delta], more = with_tables(
            functools.partial(exchange, delta=delta), line[last], tables, delta
        )
        tables = tables | more
        delta //= 2
    held = list(line)
    chunks = dict(line)
    chunks[PAIR] = beside
    for k in held[1:-1]:
        chunks[k ^ PAIR] = exchange(line[k], PAIR)
    last = held[-1]
    chunks[last ^ PAIR], more = with_tables(
        functools.partial(exchange, delta=PAIR), line[last], tables, PAIR
    )
    tables = tables | more
    return chunks, tables


def swap_cores(chunks, tables):
    keys = list(chunks)
    early, late = keys[: len(keys) // 2], keys[len(keys) // 2 :]
    groups = []
    first = exchange(jnp.concatenate([chunks[k] for k in early]), CORE)
    second = exchange(jnp.concatenate([chunks[k] for k in late]), CORE)
    names = list(tables)
    other = exchange(jnp.concatenate([tables[k] for k in names], axis=1), CORE)
    each = tables[names[0]].shape[1]
    for n, k in enumerate(names):
        tables = tables | {k ^ CORE: other[:, n * each : (n + 1) * each]}
    groups += [([k], chunks[k]) for k in keys]
    groups += [([k ^ CORE for k in early], first), ([k ^ CORE for k in late], second)]
    return groups, tables


def slot_units(order, most):
    blocks = max(1, ROWS // most)
    return blocks, list(dict.fromkeys(delta // blocks for delta in order))


def slot_bases(order, most, tok, me):
    blocks, units = slot_units(order, most)
    deltas = jnp.asarray(order, jnp.int32)
    starts = jnp.asarray([units.index(delta // blocks) * blocks * most for delta in order], jnp.int32)
    return jnp.repeat(starts + (me ^ deltas) % blocks * most, tok)[None, :]


def down_kernel(order, most, tok, *refs):
    me_ref, base_ref, table_ref, saved_ref, w_ref = refs[:5]
    token_refs, (out_ref, x_ref, d_ref) = refs[5:-3], refs[-3:]
    width = w_ref.shape[0]
    slots = saved_ref.shape[0]
    count = len(order) * tok
    blocks, units = slot_units(order, most)
    tall = blocks * most
    me = me_ref[0]
    at = 0
    for ref in token_refs:
        x_ref[at : at + ref.shape[0], :] = ref[...]
        at += ref.shape[0]
    experts = table_ref.shape[1] // 2
    lanes = lax.broadcasted_iota(jnp.int32, (8, 2 * experts), 1)
    pick = jnp.where((lanes == me) | (lanes == me + experts), 1.0, 0.0).astype(jnp.bfloat16)
    contract_last = (((1,), (1,)), ((), ()))
    gate = lax.dot_general(pick, table_ref[...], contract_last, preferred_element_type=jnp.float32)
    live = gate > 0.0
    rows = lax.broadcasted_iota(jnp.int32, (count, count), 0)
    cols = lax.broadcasted_iota(jnp.int32, (count, count), 1)
    earlier = jnp.where((rows < cols) & (rows // tok == cols // tok), 1.0, 0.0).astype(jnp.bfloat16)
    before = lax.dot_general(
        jnp.where(live, 1.0, 0.0).astype(jnp.bfloat16),
        earlier,
        (((1,), (0,)), ((), ())),
        preferred_element_type=jnp.float32,
    )
    slot = jnp.where(live[:1], base_ref[...] + before[:1].astype(jnp.int32), -1)
    hit = lax.broadcasted_iota(jnp.int32, (slots, count), 0) == slot
    weight = jnp.sum(jnp.where(hit, gate[:1], 0.0), axis=1, keepdims=True)
    onehot = jnp.where(hit, 1.0, 0.0).astype(jnp.bfloat16)
    step = 512 if x_ref.shape[1] % 512 == 0 else x_ref.shape[1]
    for k in range(0, x_ref.shape[1], step):
        taken = jnp.dot(onehot, x_ref[:, k : k + step], preferred_element_type=jnp.float32)
        d_ref[:, k : k + step] = (weight * taken).astype(jnp.bfloat16)
    wide = 256 if width % 256 == 0 else width
    for n in range(0, width, wide):
        hidden = lax.dot_general(
            d_ref[...], w_ref[n : n + wide, :], contract_last, preferred_element_type=jnp.float32
        )
        for i, delta in enumerate(units):
            place = pl.ds(pl.multiple_of((me // blocks ^ delta) * tall, tall), tall)
            h = hidden[i * tall : (i + 1) * tall]
            a = saved_ref[place, n : n + wide].astype(jnp.float32)
            u = saved_ref[place, width + n : width + n + wide].astype(jnp.float32)
            sig = jax.nn.sigmoid(a)
            hs = h * sig
            out_ref[place, n : n + wide] = (hs * u * (1.0 + a * (1.0 - sig))).astype(out_ref.dtype)
            out_ref[place, width + n : width + n + wide] = (hs * a).astype(out_ref.dtype)


def per_device(next_grad, routes, gates, saved, w_down):
    experts = lax.axis_size("expert")
    slots = saved.shape[2]
    most = slots // experts
    tok, features = next_grad.shape[1:]
    table = assign_table(routes[0], gates[0], experts)
    chunks, tables = gather_tokens(next_grad[0], table)
    groups, tables = swap_cores(chunks, tables)
    order = [k for keys, _ in groups for k in keys]
    table = jnp.concatenate([tables[k] for k in order])
    me = lax.axis_index("expert").astype(jnp.int32).reshape(1)
    vmem = pl.BlockSpec(memory_space=pltpu.VMEM)
    out = pl.pallas_call(
        functools.partial(down_kernel, order, most, tok),
        out_shape=jax.ShapeDtypeStruct(saved.shape[2:], jnp.bfloat16),
        in_specs=[pl.BlockSpec(memory_space=pltpu.SMEM)] + [vmem] * (4 + len(groups)),
        out_specs=vmem,
        scratch_shapes=[
            pltpu.VMEM((experts * tok, features), jnp.bfloat16),
            pltpu.VMEM((slots, features), jnp.bfloat16),
        ],
        compiler_params=pltpu.CompilerParams(vmem_limit_bytes=32 * MIB),
    )(me, slot_bases(order, most, tok, me), table, saved[0, 0], w_down[0], *[g for _, g in groups])
    return out[None, None]


def solution(mesh):
    return jax.shard_map(
        per_device,
        mesh=mesh,
        in_specs=(
            P("section", "expert", None),
            P("section", "expert", None),
            P("section", "expert", None),
            P("section", "expert", None, None),
            P("expert", None, None),
        ),
        out_specs=P("section", "expert", None, None),
        check_vma=False,
    )
```

```python
import functools

import jax
import jax.numpy as jnp
from jax import lax
from jax.experimental import pallas as pl
from jax.experimental.pallas import tpu as pltpu
from jax.sharding import PartitionSpec as P

in_space = pltpu.with_memory_space_constraint

CORE = 1
PAIR = 2
ROWS = 16
W_PARTS = 4
W_LOADS = 8
MIB = 1024 * 1024


def exchange(x, delta):
    peers = lax.axis_size("expert")
    return lax.ppermute(x, "expert", [(i, i ^ delta) for i in range(peers)])


def from_next_section(x, delta):
    sections, peers = lax.axis_size("section"), lax.axis_size("expert")
    pairs = [
        (s * peers + i, (s - 1) % sections * peers + (i ^ delta))
        for s in range(sections)
        for i in range(peers)
    ]
    return lax.ppermute(x, ("section", "expert"), pairs)


def table_kernel(routes_ref, gates_ref, out_ref):
    tok, experts = out_ref.shape[0], out_ref.shape[1] // 2
    ids = lax.broadcasted_iota(jnp.int32, (tok, experts), 1)
    table = jnp.zeros((tok, experts), jnp.float32)
    for k in range(routes_ref.shape[1]):
        table += jnp.where(routes_ref[:, k : k + 1] == ids, gates_ref[:, k : k + 1], 0.0)
    high = table.astype(jnp.bfloat16)
    out_ref[:, :experts] = high
    out_ref[:, experts:] = (table - high.astype(jnp.float32)).astype(jnp.bfloat16)


def assign_table(routes, gates, experts):
    vmem = pl.BlockSpec(memory_space=pltpu.VMEM)
    return pl.pallas_call(
        table_kernel,
        out_shape=jax.ShapeDtypeStruct((routes.shape[0], 2 * experts), jnp.bfloat16),
        in_specs=[vmem, vmem],
        out_specs=vmem,
        compiler_params=pltpu.CompilerParams(vmem_limit_bytes=MIB),
    )(routes, gates)


def with_tables(send, chunk, tables, delta):
    width = chunk.shape[1]
    keys = list(tables)
    got = send(jnp.concatenate([chunk] + [tables[k] for k in keys], axis=1))
    each = tables[keys[0]].shape[1]
    rest = {k ^ delta: got[:, width + n * each : width + (n + 1) * each] for n, k in enumerate(keys)}
    return got[:, :width], rest


def gather_tokens(grad, table):
    peers = lax.axis_size("expert")
    top = peers // 2
    far, near = from_next_section(grad, top), from_next_section(grad, 0)
    beside = from_next_section(grad, PAIR)
    tables = {0: table, top: exchange(table, top)}
    chunks = {0: near, top: far}
    delta = top // 2
    while delta > PAIR:
        held = list(chunks)
        for k in held:
            if k == 0:
                chunks[k ^ delta], more = with_tables(
                    functools.partial(exchange, delta=delta), chunks[k], tables, delta
                )
            else:
                chunks[k ^ delta] = exchange(chunks[k], delta)
        tables = tables | more
        delta //= 2
    line = list(chunks)
    chunks[PAIR] = beside
    for k in line[1:]:
        if k == 4:
            chunks[k ^ PAIR], more = with_tables(
                functools.partial(exchange, delta=PAIR), chunks[k], tables, PAIR
            )
        else:
            chunks[k ^ PAIR] = exchange(chunks[k], PAIR)
    return chunks, tables | more


def swap_cores(chunks, tables, early):
    late = [k for k in chunks if k not in early]
    groups = []
    for part in (early, late):
        own = jnp.concatenate([chunks[k] for k in part])
        groups += [(part, own), ([k ^ CORE for k in part], exchange(own, CORE))]
    names = list(tables)
    own = jnp.concatenate([tables[k] for k in names], axis=1)
    return groups, [(names, own), ([k ^ CORE for k in names], exchange(own, CORE))]


def slot_units(order, most):
    blocks = max(1, ROWS // most)
    return blocks, list(dict.fromkeys(delta // blocks for delta in order))


def slot_bases(order, most, tok, me):
    blocks, units = slot_units(order, most)
    deltas = jnp.asarray(order, jnp.int32)
    starts = jnp.asarray([units.index(delta // blocks) * blocks * most for delta in order], jnp.int32)
    return jnp.repeat(starts + (me ^ deltas) % blocks * most, tok)[None, :]


def down_kernel(order, table_order, most, tok, *refs):
    me_ref, base_ref, saved_hbm, w_hbm = refs[:4]
    table_refs = refs[4 : 4 + len(table_order)]
    token_refs = refs[4 + len(table_order) : -7]
    out_ref, x_ref, d_ref, table_ref, saved_ref, w_ref, sems = refs[-7:]
    width = w_ref.shape[0]
    slots = saved_ref.shape[0]
    count = len(order) * tok
    blocks, units = slot_units(order, most)
    tall = blocks * most
    me = me_ref[0]
    height = width // W_LOADS

    def load(n):
        part = pl.ds(pl.multiple_of(n * height, height), height)
        return pltpu.make_async_copy(w_hbm.at[part], w_ref.at[part], sems.at[n])

    saved_load = pltpu.make_async_copy(saved_hbm, saved_ref, sems.at[W_LOADS])
    for n in range(W_LOADS):
        load(n).start()
        if n == 0:
            saved_load.start()
    at = 0
    for ref in token_refs:
        x_ref[at : at + ref.shape[0], :] = ref[...]
        at += ref.shape[0]
    experts = table_ref.shape[1] // 2
    for names, ref in zip(table_order, table_refs, strict=True):
        for n, k in enumerate(names):
            i = order.index(k)
            table_ref[i * tok : (i + 1) * tok, :] = ref[:, n * 2 * experts : (n + 1) * 2 * experts]
    lanes = lax.broadcasted_iota(jnp.int32, (8, 2 * experts), 1)
    pick = jnp.where((lanes == me) | (lanes == me + experts), 1.0, 0.0).astype(jnp.bfloat16)
    contract_last = (((1,), (1,)), ((), ()))
    gate = lax.dot_general(pick, table_ref[...], contract_last, preferred_element_type=jnp.float32)
    live = gate > 0.0
    rows = lax.broadcasted_iota(jnp.int32, (count, count), 0)
    cols = lax.broadcasted_iota(jnp.int32, (count, count), 1)
    earlier = jnp.where((rows < cols) & (rows // tok == cols // tok), 1.0, 0.0).astype(jnp.bfloat16)
    before = lax.dot_general(
        jnp.where(live, 1.0, 0.0).astype(jnp.bfloat16),
        earlier,
        (((1,), (0,)), ((), ())),
        preferred_element_type=jnp.float32,
    )
    slot = jnp.where(live[:1], base_ref[...] + before[:1].astype(jnp.int32), -1)
    hit = lax.broadcasted_iota(jnp.int32, (slots, count), 0) == slot
    weight = jnp.sum(jnp.where(hit, gate[:1], 0.0), axis=1, keepdims=True)
    onehot = jnp.where(hit, 1.0, 0.0).astype(jnp.bfloat16)
    step = 512 if x_ref.shape[1] % 512 == 0 else x_ref.shape[1]
    for k in range(0, x_ref.shape[1], step):
        taken = jnp.dot(onehot, x_ref[:, k : k + step], preferred_element_type=jnp.float32)
        d_ref[:, k : k + step] = (weight * taken).astype(jnp.bfloat16)
    saved_load.wait()
    wide = width // W_PARTS

    @pl.loop(0, W_PARTS)
    def _(part):
        for n in range(W_LOADS // W_PARTS):
            load(part * (W_LOADS // W_PARTS) + n).wait()
        at = pl.multiple_of(part * wide, wide)
        hidden = lax.dot_general(
            d_ref[...], w_ref[pl.ds(at, wide), :], contract_last, preferred_element_type=jnp.float32
        )
        for i, delta in enumerate(units):
            place = pl.ds(pl.multiple_of((me // blocks ^ delta) * tall, tall), tall)
            h = hidden[i * tall : (i + 1) * tall]
            a = saved_ref[place, pl.ds(at, wide)].astype(jnp.float32)
            u = saved_ref[place, pl.ds(width + at, wide)].astype(jnp.float32)
            sig = jax.nn.sigmoid(a)
            hs = h * sig
            out_ref[place, pl.ds(at, wide)] = (hs * u * (1.0 + a * (1.0 - sig))).astype(out_ref.dtype)
            out_ref[place, pl.ds(width + at, wide)] = (hs * a).astype(out_ref.dtype)


def per_device(next_grad, routes, gates, saved, w_down):
    experts = lax.axis_size("expert")
    most = saved.shape[2] // experts
    tok, features = next_grad.shape[1:]
    table = assign_table(routes[0], gates[0], experts)
    chunks, tables = gather_tokens(next_grad[0], table)
    groups, tables = swap_cores(chunks, tables, [0, 8, 4, 2, 10])
    order = [k for keys, _ in groups for k in keys]
    me = lax.axis_index("expert").astype(jnp.int32).reshape(1)
    vmem, hbm = pl.BlockSpec(memory_space=pltpu.VMEM), pl.BlockSpec(memory_space=pl.ANY)
    out = pl.pallas_call(
        functools.partial(down_kernel, order, [names for names, _ in tables], most, tok),
        out_shape=jax.ShapeDtypeStruct(saved.shape[2:], jnp.bfloat16),
        in_specs=[pl.BlockSpec(memory_space=pltpu.SMEM), vmem, hbm, hbm]
        + [vmem] * (len(tables) + len(groups)),
        out_specs=vmem,
        scratch_shapes=[
            pltpu.VMEM((experts * tok, features), jnp.bfloat16),
            pltpu.VMEM((saved.shape[2], features), jnp.bfloat16),
            pltpu.VMEM((experts * tok, 2 * experts), jnp.bfloat16),
            pltpu.VMEM(saved.shape[2:], jnp.bfloat16),
            pltpu.VMEM(w_down.shape[1:], jnp.bfloat16),
            pltpu.SemaphoreType.DMA((W_LOADS + 1,)),
        ],
        compiler_params=pltpu.CompilerParams(vmem_limit_bytes=40 * MIB),
    )(
        me,
        slot_bases(order, most, tok, me),
        in_space(saved[0, 0], pltpu.HBM),
        in_space(w_down[0], pltpu.HBM),
        *[t for _, t in tables],
        *[g for _, g in groups],
    )
    return out[None, None]


def solution(mesh):
    return jax.shard_map(
        per_device,
        mesh=mesh,
        in_specs=(
            P("section", "expert", None),
            P("section", "expert", None),
            P("section", "expert", None),
            P("section", "expert", None, None),
            P("expert", None, None),
        ),
        out_specs=P("section", "expert", None, None),
        check_vma=False,
    )
```

```python
import functools

import jax
import jax.numpy as jnp
from jax import lax
from jax.experimental import pallas as pl
from jax.experimental.pallas import tpu as pltpu
from jax.sharding import PartitionSpec as P

in_space = pltpu.with_memory_space_constraint

CORE = 1
PAIR = 2
ROWS = 16
W_PARTS = 4
W_LOADS = 2
FIRST_LOADS = 4
MIB = 1024 * 1024
CONTRACT_LAST = (((1,), (1,)), ((), ()))


def exchange(x, delta):
    peers = lax.axis_size("expert")
    return lax.ppermute(x, "expert", [(i, i ^ delta) for i in range(peers)])


def from_next_section(x, delta):
    sections, peers = lax.axis_size("section"), lax.axis_size("expert")
    pairs = [
        (s * peers + i, (s - 1) % sections * peers + (i ^ delta))
        for s in range(sections)
        for i in range(peers)
    ]
    return lax.ppermute(x, ("section", "expert"), pairs)


def table_kernel(routes_hbm, gates_hbm, saved_hbm, out_ref, saved_ref, routes_ref, gates_ref, sems):
    loads = [
        pltpu.make_async_copy(routes_hbm, routes_ref, sems.at[0]),
        pltpu.make_async_copy(gates_hbm, gates_ref, sems.at[1]),
        pltpu.make_async_copy(saved_hbm, saved_ref, sems.at[2]),
    ]
    for load in loads:
        load.start()
    for load in loads[:2]:
        load.wait()
    tok, experts = out_ref.shape[0], out_ref.shape[1] // 2
    ids = lax.broadcasted_iota(jnp.int32, (experts, tok), 0)
    table = jnp.zeros((experts, tok), jnp.float32)
    for k in range(routes_ref.shape[0]):
        table += jnp.where(routes_ref[k : k + 1, :] == ids, gates_ref[k : k + 1, :], 0.0)
    table = table.T
    high = table.astype(jnp.bfloat16)
    out_ref[:, :experts] = high
    out_ref[:, experts:] = (table - high.astype(jnp.float32)).astype(jnp.bfloat16)
    loads[2].wait()


def assign_table(routes, gates, saved, experts):
    vmem, hbm = pl.BlockSpec(memory_space=pltpu.VMEM), pl.BlockSpec(memory_space=pl.ANY)
    return pl.pallas_call(
        table_kernel,
        out_shape=[
            jax.ShapeDtypeStruct((routes.shape[0], 2 * experts), jnp.bfloat16),
            jax.ShapeDtypeStruct(saved.shape, saved.dtype),
        ],
        in_specs=[hbm] * 3,
        out_specs=[vmem] * 2,
        scratch_shapes=[
            pltpu.VMEM(routes.shape[::-1], routes.dtype),
            pltpu.VMEM(gates.shape[::-1], gates.dtype),
            pltpu.SemaphoreType.DMA((3,)),
        ],
        compiler_params=pltpu.CompilerParams(vmem_limit_bytes=MIB),
    )(*[in_space(x, pltpu.HBM) for x in (routes.T, gates.T, saved)])


def join_kernel(count, *refs):
    out_ref = refs[-1]
    at = 0
    for ref in refs[:count]:
        out_ref[:, at : at + ref.shape[1]] = ref[...]
        at += ref.shape[1]


def join(parts, after=()):
    vmem, hbm = pl.BlockSpec(memory_space=pltpu.VMEM), pl.BlockSpec(memory_space=pl.ANY)
    width = sum(part.shape[1] for part in parts)
    return pl.pallas_call(
        functools.partial(join_kernel, len(parts)),
        out_shape=jax.ShapeDtypeStruct((parts[0].shape[0], width), parts[0].dtype),
        in_specs=[vmem] * len(parts) + [hbm] * len(after),
        out_specs=vmem,
        compiler_params=pltpu.CompilerParams(vmem_limit_bytes=4 * MIB),
    )(*parts, *after)


def gather_tokens(grad, table):
    peers = lax.axis_size("expert")
    top = peers // 2
    middle = [1 << b for b in reversed(range(2, top.bit_length() - 1))]
    width = grad.shape[1]
    names, tables = [0], table

    def add_tables(got, delta):
        nonlocal names, tables
        names, tables = names + [k ^ delta for k in names], jnp.concatenate([tables, got], axis=1)

    def with_tables(k, delta, after=()):
        got = exchange(join([chunks[k], tables], after), delta)
        chunks[k ^ delta] = got[:, :width]
        add_tables(got[:, width:], delta)

    near, far = [0], [top]
    for delta in middle:
        near += [k ^ delta for k in near]
    chunks = {k: from_next_section(grad, k) for k in [PAIR] + near[1:] + [top, 0]}
    add_tables(exchange(tables, top), top)
    for delta in middle:
        for k in far[:-1]:
            chunks[k ^ delta] = exchange(chunks[k], delta)
        with_tables(far[-1], delta)
        far += [k ^ delta for k in far]
    rest = far + near[1:]
    for k in rest[:-1]:
        chunks[k ^ PAIR] = exchange(chunks[k], PAIR)
    with_tables(rest[-1], PAIR, after=[chunks[PAIR]])
    late = [k ^ PAIR for k in far]
    return chunks, late, [(names, tables), ([k ^ CORE for k in names], exchange(tables, CORE))]


def swap_cores(chunks, late):
    groups = []
    for part in ([k for k in chunks if k not in late], late):
        own = jnp.concatenate([chunks[k] for k in part])
        groups += [(part, own), ([k ^ CORE for k in part], exchange(own, CORE))]
    return groups


def slot_units(order, most):
    blocks = max(1, ROWS // most)
    return blocks, list(dict.fromkeys(delta // blocks for delta in order))


def slot_bases(order, most, tok, me):
    blocks, units = slot_units(order, most)
    deltas = jnp.asarray(order, jnp.int32)
    starts = jnp.asarray([units.index(delta // blocks) * blocks * most for delta in order], jnp.int32)
    return jnp.repeat(starts + (me ^ deltas) % blocks * most, tok)[None, :]


def find_slots(order, table_order, tok, me, base_ref, table_refs, table_ref):
    experts = table_ref.shape[1] // 2
    count = len(order) * tok
    for names, ref in zip(table_order, table_refs, strict=True):
        for n, k in enumerate(names):
            i = order.index(k)
            table_ref[i * tok : (i + 1) * tok, :] = ref[:, n * 2 * experts : (n + 1) * 2 * experts]
    lanes = lax.broadcasted_iota(jnp.int32, (8, 2 * experts), 1)
    pick = jnp.where((lanes == me) | (lanes == me + experts), 1.0, 0.0).astype(jnp.bfloat16)
    gate = lax.dot_general(pick, table_ref[...], CONTRACT_LAST, preferred_element_type=jnp.float32)
    live = gate > 0.0
    rows = lax.broadcasted_iota(jnp.int32, (count, count), 0)
    cols = lax.broadcasted_iota(jnp.int32, (count, count), 1)
    earlier = jnp.where((rows < cols) & (rows // tok == cols // tok), 1.0, 0.0).astype(jnp.bfloat16)
    before = lax.dot_general(
        jnp.where(live, 1.0, 0.0).astype(jnp.bfloat16),
        earlier,
        (((1,), (0,)), ((), ())),
        preferred_element_type=jnp.float32,
    )
    slot = jnp.where(live[:1], base_ref[...] + before[:1].astype(jnp.int32), -1)
    return slot, gate[:1]


def fill_rows(out_ref, token_ref, slot, gate, first, height, add=False):
    hit = first + lax.broadcasted_iota(jnp.int32, (height, slot.shape[1]), 0) == slot
    weight = jnp.sum(jnp.where(hit, gate, 0.0), axis=1, keepdims=True)
    onehot = jnp.where(hit, 1.0, 0.0).astype(jnp.bfloat16)
    width = token_ref.shape[1]
    step = 512 if width % 512 == 0 else width
    for k in range(0, width, step):
        taken = jnp.dot(onehot, token_ref[:, k : k + step], preferred_element_type=jnp.float32)
        scaled = (weight * taken).astype(out_ref.dtype)
        if add:
            scaled += out_ref[first : first + height, k : k + step]
        out_ref[first : first + height, k : k + step] = scaled


def down_kernel(order, table_order, tok, most, me_ref, base_ref, saved_ref, w_hbm, *refs):
    table_refs, token_refs = refs[: len(table_order)], refs[len(table_order) : -7]
    out_hbm, d_ref, w_ref, out_ref, table_ref, sems, out_sems = refs[-7:]
    width = w_ref.shape[0]
    blocks, units = slot_units(order, most)
    tall = blocks * most
    me = me_ref[0]
    wide = width // W_PARTS
    height = wide // W_LOADS

    def load(n):
        part = pl.ds(pl.multiple_of(n * height, height), height)
        return pltpu.make_async_copy(w_hbm.at[part], w_ref.at[part], sems.at[n])

    def stores(part):
        for half in range(2):
            span = pl.ds(pl.multiple_of(half * width + part * wide, wide), wide)
            yield pltpu.make_async_copy(out_ref.at[:, span], out_hbm.at[:, span], out_sems.at[2 * part + half])

    for n in range(FIRST_LOADS):
        load(n).start()
    slot, gate = find_slots(order, table_order, tok, me, base_ref, table_refs, table_ref)
    token, row = 0, 0
    for ref in token_refs:
        count = ref.shape[0]
        size = count // tok * most
        span = slice(token, token + count)
        if blocks == 1:
            fill_rows(d_ref, ref, slot[:, span], gate[:, span], row, size)
        else:
            fill_rows(d_ref, ref, slot[:, span], gate[:, span], 0, d_ref.shape[0], add=token > 0)
        token, row = token + count, row + size
    for n in range(FIRST_LOADS, W_PARTS * W_LOADS):
        load(n).start()

    @pl.loop(0, W_PARTS)
    def _(part):
        for n in range(W_LOADS):
            load(part * W_LOADS + n).wait()
        at = pl.multiple_of(part * wide, wide)
        hidden = lax.dot_general(
            d_ref[...], w_ref[pl.ds(at, wide), :], CONTRACT_LAST, preferred_element_type=jnp.float32
        )
        for i, delta in enumerate(units):
            place = pl.ds(pl.multiple_of((me // blocks ^ delta) * tall, tall), tall)
            h = hidden[i * tall : (i + 1) * tall]
            a = saved_ref[place, pl.ds(at, wide)].astype(jnp.float32)
            u = saved_ref[place, pl.ds(width + at, wide)].astype(jnp.float32)
            sig = jax.nn.sigmoid(a)
            hs = h * sig
            out_ref[place, pl.ds(at, wide)] = (hs * u * (1.0 + a * (1.0 - sig))).astype(out_ref.dtype)
            out_ref[place, pl.ds(width + at, wide)] = (hs * a).astype(out_ref.dtype)
        for store in stores(part):
            store.start()

    for part in range(W_PARTS):
        for store in stores(part):
            store.wait()


def per_device(next_grad, routes, gates, saved, w_down):
    experts = lax.axis_size("expert")
    slots, width = saved.shape[2:]
    most = slots // experts
    tok, features = next_grad.shape[1:]
    table, near_saved = assign_table(routes[0], gates[0], saved[0, 0], experts)
    chunks, late, tables = gather_tokens(next_grad[0], table)
    groups = swap_cores(chunks, late)
    order = [k for names, _ in groups for k in names]
    me = lax.axis_index("expert").astype(jnp.int32).reshape(1)
    smem = pl.BlockSpec(memory_space=pltpu.SMEM)
    vmem, hbm = pl.BlockSpec(memory_space=pltpu.VMEM), pl.BlockSpec(memory_space=pl.ANY)
    out = pl.pallas_call(
        functools.partial(down_kernel, order, [names for names, _ in tables], tok, most),
        out_shape=jax.ShapeDtypeStruct((slots, width), jnp.bfloat16),
        in_specs=[smem, vmem, vmem, hbm] + [vmem] * (len(tables) + len(groups)),
        out_specs=hbm,
        scratch_shapes=[
            pltpu.VMEM((slots, features), jnp.bfloat16),
            pltpu.VMEM(w_down.shape[1:], jnp.bfloat16),
            pltpu.VMEM((slots, width), jnp.bfloat16),
            pltpu.VMEM((experts * tok, 2 * experts), jnp.bfloat16),
            pltpu.SemaphoreType.DMA((W_PARTS * W_LOADS,)),
            pltpu.SemaphoreType.DMA((2 * W_PARTS,)),
        ],
        compiler_params=pltpu.CompilerParams(vmem_limit_bytes=40 * MIB),
    )(
        me,
        slot_bases(order, most, tok, me),
        near_saved,
        in_space(w_down[0], pltpu.HBM),
        *[array for _, array in tables],
        *[array for _, array in groups],
    )
    return out[None, None]


def solution(mesh):
    return jax.shard_map(
        per_device,
        mesh=mesh,
        in_specs=(
            P("section", "expert", None),
            P("section", "expert", None),
            P("section", "expert", None),
            P("section", "expert", None, None),
            P("expert", None, None),
        ),
        out_specs=P("section", "expert", None, None),
        check_vma=False,
    )
```

```python
import functools

import jax
import jax.numpy as jnp
from jax import lax
from jax.experimental import pallas as pl
from jax.experimental.pallas import tpu as pltpu
from jax.sharding import PartitionSpec as P

in_space = pltpu.with_memory_space_constraint

CORE = 1
PAIR = 2
ROWS = 16
W_PARTS = 4
W_LOADS = 2
MIB = 1024 * 1024
CONTRACT_LAST = (((1,), (1,)), ((), ()))


def exchange(x, delta):
    peers = lax.axis_size("expert")
    return lax.ppermute(x, "expert", [(i, i ^ delta) for i in range(peers)])


def from_next_section(x, delta):
    sections, peers = lax.axis_size("section"), lax.axis_size("expert")
    pairs = [
        (s * peers + i, (s - 1) % sections * peers + (i ^ delta))
        for s in range(sections)
        for i in range(peers)
    ]
    return lax.ppermute(x, ("section", "expert"), pairs)


def table_kernel(routes_hbm, gates_hbm, saved_hbm, out_ref, saved_ref, routes_ref, gates_ref, sems):
    loads = [
        pltpu.make_async_copy(routes_hbm, routes_ref, sems.at[0]),
        pltpu.make_async_copy(gates_hbm, gates_ref, sems.at[1]),
        pltpu.make_async_copy(saved_hbm, saved_ref, sems.at[2]),
    ]
    for load in loads:
        load.start()
    for load in loads[:2]:
        load.wait()
    tok, experts = out_ref.shape[0], out_ref.shape[1] // 2
    ids = lax.broadcasted_iota(jnp.int32, (experts, tok), 0)
    table = jnp.zeros((experts, tok), jnp.float32)
    for k in range(routes_ref.shape[0]):
        table += jnp.where(routes_ref[k : k + 1, :] == ids, gates_ref[k : k + 1, :], 0.0)
    table = table.T
    high = table.astype(jnp.bfloat16)
    out_ref[:, :experts] = high
    out_ref[:, experts:] = (table - high.astype(jnp.float32)).astype(jnp.bfloat16)
    loads[2].wait()


def assign_table(routes, gates, saved, experts):
    vmem, hbm = pl.BlockSpec(memory_space=pltpu.VMEM), pl.BlockSpec(memory_space=pl.ANY)
    return pl.pallas_call(
        table_kernel,
        out_shape=[
            jax.ShapeDtypeStruct((routes.shape[0], 2 * experts), jnp.bfloat16),
            jax.ShapeDtypeStruct(saved.shape, saved.dtype),
        ],
        in_specs=[hbm] * 3,
        out_specs=[vmem] * 2,
        scratch_shapes=[
            pltpu.VMEM(routes.shape[::-1], routes.dtype),
            pltpu.VMEM(gates.shape[::-1], gates.dtype),
            pltpu.SemaphoreType.DMA((3,)),
        ],
        compiler_params=pltpu.CompilerParams(vmem_limit_bytes=MIB),
    )(*[in_space(x, pltpu.HBM) for x in (routes.T, gates.T, saved)])


def join_kernel(count, *refs):
    out_ref = refs[-1]
    at = 0
    for ref in refs[:count]:
        out_ref[:, at : at + ref.shape[1]] = ref[...]
        at += ref.shape[1]


def join(parts, after=()):
    vmem, hbm = pl.BlockSpec(memory_space=pltpu.VMEM), pl.BlockSpec(memory_space=pl.ANY)
    width = sum(part.shape[1] for part in parts)
    return pl.pallas_call(
        functools.partial(join_kernel, len(parts)),
        out_shape=jax.ShapeDtypeStruct((parts[0].shape[0], width), parts[0].dtype),
        in_specs=[vmem] * len(parts) + [hbm] * len(after),
        out_specs=vmem,
        compiler_params=pltpu.CompilerParams(vmem_limit_bytes=4 * MIB),
    )(*parts, *after)


def gather_tokens(grad, table):
    peers = lax.axis_size("expert")
    top = peers // 2
    middle = [1 << b for b in reversed(range(2, top.bit_length() - 1))]
    width = grad.shape[1]
    names, tables = [0], table

    def add_tables(got, delta):
        nonlocal names, tables
        names, tables = names + [k ^ delta for k in names], jnp.concatenate([tables, got], axis=1)

    def with_tables(k, delta, after=()):
        got = exchange(join([chunks[k], tables], after), delta)
        chunks[k ^ delta] = got[:, :width]
        add_tables(got[:, width:], delta)

    near, far = [0], [top]
    for delta in middle:
        near += [k ^ delta for k in near]
    chunks = {k: from_next_section(grad, k) for k in [PAIR] + near[1:] + [top, 0]}
    add_tables(exchange(tables, top), top)
    for delta in middle:
        for k in far[:-1]:
            chunks[k ^ delta] = exchange(chunks[k], delta)
        with_tables(far[-1], delta)
        far += [k ^ delta for k in far]
    rest = far + near[1:]
    for k in rest[:-1]:
        chunks[k ^ PAIR] = exchange(chunks[k], PAIR)
    with_tables(rest[-1], PAIR, after=[chunks[PAIR]])
    late = [near[-1] ^ PAIR, far[-1] ^ PAIR]
    return chunks, late, [(names, tables), ([k ^ CORE for k in names], exchange(tables, CORE))]


def swap_cores(chunks, late, waits):
    early = [k for k in chunks if k not in late]
    groups = []
    for part, after in ((early, ()), (late, waits)):
        own = jnp.concatenate([chunks[k] for k in part])
        if after:
            own = join([own], after=after)
        groups.append([(part, own), ([k ^ CORE for k in part], exchange(own, CORE))])
    return groups


def slot_units(order, most):
    blocks = -(-ROWS // most)
    return blocks, list(dict.fromkeys(delta // blocks for delta in order))


def slot_bases(order, most, tok, me):
    blocks, units = slot_units(order, most)
    deltas = jnp.asarray(order, jnp.int32)
    starts = jnp.asarray([units.index(delta // blocks) * blocks * most for delta in order], jnp.int32)
    return jnp.repeat(starts + (me ^ deltas) % blocks * most, tok)[None, :]


def find_slots(order, table_order, tok, me, base_ref, table_refs, table_ref):
    experts = table_ref.shape[1] // 2
    count = len(order) * tok
    for names, ref in zip(table_order, table_refs, strict=True):
        for n, k in enumerate(names):
            i = order.index(k)
            table_ref[i * tok : (i + 1) * tok, :] = ref[:, n * 2 * experts : (n + 1) * 2 * experts]
    lanes = lax.broadcasted_iota(jnp.int32, (8, 2 * experts), 1)
    pick = jnp.where((lanes == me) | (lanes == me + experts), 1.0, 0.0).astype(jnp.bfloat16)
    gate = lax.dot_general(pick, table_ref[...], CONTRACT_LAST, preferred_element_type=jnp.float32)
    live = gate > 0.0
    rows = lax.broadcasted_iota(jnp.int32, (count, count), 0)
    cols = lax.broadcasted_iota(jnp.int32, (count, count), 1)
    earlier = jnp.where((rows < cols) & (rows // tok == cols // tok), 1.0, 0.0).astype(jnp.bfloat16)
    before = lax.dot_general(
        jnp.where(live, 1.0, 0.0).astype(jnp.bfloat16),
        earlier,
        (((1,), (0,)), ((), ())),
        preferred_element_type=jnp.float32,
    )
    slot = jnp.where(live[:1], base_ref[...] + before[:1].astype(jnp.int32), -1)
    return slot, gate[:1]


def fill_rows(out_ref, token_ref, slot, gate, first, height, add=False):
    hit = first + lax.broadcasted_iota(jnp.int32, (height, slot.shape[1]), 0) == slot
    weight = jnp.sum(jnp.where(hit, gate, 0.0), axis=1, keepdims=True)
    onehot = jnp.where(hit, 1.0, 0.0).astype(jnp.bfloat16)
    width = token_ref.shape[1]
    step = 512 if width % 512 == 0 else width
    for k in range(0, width, step):
        taken = jnp.dot(onehot, token_ref[:, k : k + step], preferred_element_type=jnp.float32)
        scaled = (weight * taken).astype(out_ref.dtype)
        if add:
            scaled += out_ref[first : first + height, k : k + step]
        out_ref[first : first + height, k : k + step] = scaled


def arrange_kernel(order, table_order, tok, most, *refs):
    me_ref, base_ref = refs[:2]
    table_refs = refs[2 : 2 + len(table_order)]
    token_refs = refs[2 + len(table_order) : -4]
    rows_ref, slot_ref, gate_ref, table_ref = refs[-4:]
    slot, gate = find_slots(order, table_order, tok, me_ref[0], base_ref, table_refs, table_ref)
    slot_ref[...] = slot
    gate_ref[...] = gate
    token, row = 0, 0
    for ref in token_refs:
        count = ref.shape[0]
        height = count // tok * most
        span = slice(token, token + count)
        if rows_ref.shape[0] < base_ref.shape[1] // tok * most:
            fill_rows(rows_ref, ref, slot[:, span], gate[:, span], row, height)
        else:
            fill_rows(rows_ref, ref, slot[:, span], gate[:, span], 0, rows_ref.shape[0], add=token > 0)
        token, row = token + count, row + height


def down_kernel(order, tok, most, me_ref, slot_ref, gate_ref, saved_ref, w_hbm, early_ref, *refs):
    token_refs, (out_hbm, d_ref, w_ref, out_ref, sems, out_sems) = refs[:-6], refs[-6:]
    width = w_ref.shape[0]
    blocks, units = slot_units(order, most)
    tall = blocks * most
    me = me_ref[0]
    wide = width // W_PARTS
    height = wide // W_LOADS

    def load(n):
        part = pl.ds(pl.multiple_of(n * height, height), height)
        return pltpu.make_async_copy(w_hbm.at[part], w_ref.at[part], sems.at[n])

    def stores(part):
        for half in range(2):
            span = pl.ds(pl.multiple_of(half * width + part * wide, wide), wide)
            yield pltpu.make_async_copy(out_ref.at[:, span], out_hbm.at[:, span], out_sems.at[2 * part + half])

    for n in range(W_PARTS * W_LOADS):
        load(n).start()
    row = early_ref.shape[0]
    d_ref[:row, :] = early_ref[...]
    token = len(order) * tok - sum(ref.shape[0] for ref in token_refs)
    for ref in token_refs:
        count = ref.shape[0]
        size = count // tok * most
        span = slice(token, token + count)
        if blocks == 1:
            fill_rows(d_ref, ref, slot_ref[:, span], gate_ref[:, span], row, size)
        else:
            fill_rows(d_ref, ref, slot_ref[:, span], gate_ref[:, span], 0, d_ref.shape[0], add=True)
        token, row = token + count, row + size

    @pl.loop(0, W_PARTS)
    def _(part):
        for n in range(W_LOADS):
            load(part * W_LOADS + n).wait()
        at = pl.multiple_of(part * wide, wide)
        hidden = lax.dot_general(
            d_ref[...], w_ref[pl.ds(at, wide), :], CONTRACT_LAST, preferred_element_type=jnp.float32
        )
        for i, delta in enumerate(units):
            place = pl.ds(pl.multiple_of((me // blocks ^ delta) * tall, tall), tall)
            h = hidden[i * tall : (i + 1) * tall]
            a = saved_ref[place, pl.ds(at, wide)].astype(jnp.float32)
            u = saved_ref[place, pl.ds(width + at, wide)].astype(jnp.float32)
            sig = jax.nn.sigmoid(a)
            hs = h * sig
            out_ref[place, pl.ds(at, wide)] = (hs * u * (1.0 + a * (1.0 - sig))).astype(out_ref.dtype)
            out_ref[place, pl.ds(width + at, wide)] = (hs * a).astype(out_ref.dtype)
        for store in stores(part):
            store.start()

    for part in range(W_PARTS):
        for store in stores(part):
            store.wait()


def per_device(next_grad, routes, gates, saved, w_down):
    experts = lax.axis_size("expert")
    slots, width = saved.shape[2:]
    most = slots // experts
    tok, features = next_grad.shape[1:]
    table, near_saved = assign_table(routes[0], gates[0], saved[0, 0], experts)
    chunks, late, tables = gather_tokens(next_grad[0], table)
    pairs = swap_cores(chunks, late, [array for _, array in tables[1:]])
    (early_own, early_other), (late_own, late_other) = pairs
    order = [k for names, _ in (early_own, early_other, late_own, late_other) for k in names]
    me = lax.axis_index("expert").astype(jnp.int32).reshape(1)
    smem = pl.BlockSpec(memory_space=pltpu.SMEM)
    vmem, hbm = pl.BlockSpec(memory_space=pltpu.VMEM), pl.BlockSpec(memory_space=pl.ANY)
    count = experts * tok
    early = early_own[1].shape[0] * 2 // tok * most if most >= ROWS else slots
    rows, slot, gate = pl.pallas_call(
        functools.partial(arrange_kernel, order, [names for names, _ in tables], tok, most),
        out_shape=[
            jax.ShapeDtypeStruct((early, features), jnp.bfloat16),
            jax.ShapeDtypeStruct((1, count), jnp.int32),
            jax.ShapeDtypeStruct((1, count), jnp.float32),
        ],
        in_specs=[smem] + [vmem] * (1 + len(tables) + 2),
        out_specs=[vmem] * 3,
        scratch_shapes=[pltpu.VMEM((count, 2 * experts), jnp.bfloat16)],
        compiler_params=pltpu.CompilerParams(vmem_limit_bytes=16 * MIB),
    )(
        me,
        slot_bases(order, most, tok, me),
        *[array for _, array in tables],
        early_own[1],
        early_other[1],
    )
    out = pl.pallas_call(
        functools.partial(down_kernel, order, tok, most),
        out_shape=jax.ShapeDtypeStruct((slots, width), jnp.bfloat16),
        in_specs=[smem, vmem, vmem, vmem, hbm, vmem, vmem, vmem],
        out_specs=hbm,
        scratch_shapes=[
            pltpu.VMEM((slots, features), jnp.bfloat16),
            pltpu.VMEM(w_down.shape[1:], jnp.bfloat16),
            pltpu.VMEM((slots, width), jnp.bfloat16),
            pltpu.SemaphoreType.DMA((W_PARTS * W_LOADS,)),
            pltpu.SemaphoreType.DMA((2 * W_PARTS,)),
        ],
        compiler_params=pltpu.CompilerParams(vmem_limit_bytes=40 * MIB),
    )(
        me,
        slot,
        gate,
        near_saved,
        in_space(w_down[0], pltpu.HBM),
        rows,
        late_own[1],
        late_other[1],
    )
    return out[None, None]


def solution(mesh):
    return jax.shard_map(
        per_device,
        mesh=mesh,
        in_specs=(
            P("section", "expert", None),
            P("section", "expert", None),
            P("section", "expert", None),
            P("section", "expert", None, None),
            P("expert", None, None),
        ),
        out_specs=P("section", "expert", None, None),
        check_vma=False,
    )
```

```python
import functools

import jax
import jax.numpy as jnp
from jax import lax
from jax.experimental import pallas as pl
from jax.experimental.pallas import tpu as pltpu
from jax.sharding import PartitionSpec as P

in_space = pltpu.with_memory_space_constraint

CORE = 1
PAIR = 2
ROWS = 16
W_PARTS = 4
W_LOADS = 2
MIB = 1024 * 1024
CONTRACT_LAST = (((1,), (1,)), ((), ()))


def exchange(x, delta):
    peers = lax.axis_size("expert")
    return lax.ppermute(x, "expert", [(i, i ^ delta) for i in range(peers)])


def from_next_section(x, delta):
    sections, peers = lax.axis_size("section"), lax.axis_size("expert")
    pairs = [
        (s * peers + i, (s - 1) % sections * peers + (i ^ delta))
        for s in range(sections)
        for i in range(peers)
    ]
    return lax.ppermute(x, ("section", "expert"), pairs)


def table_kernel(routes_hbm, gates_hbm, saved_hbm, out_ref, saved_ref, routes_ref, gates_ref, sems):
    loads = [
        pltpu.make_async_copy(routes_hbm, routes_ref, sems.at[0]),
        pltpu.make_async_copy(gates_hbm, gates_ref, sems.at[1]),
        pltpu.make_async_copy(saved_hbm, saved_ref, sems.at[2]),
    ]
    for load in loads:
        load.start()
    for load in loads[:2]:
        load.wait()
    tok, experts = out_ref.shape[0], out_ref.shape[1] // 2
    ids = lax.broadcasted_iota(jnp.int32, (experts, tok), 0)
    table = jnp.zeros((experts, tok), jnp.float32)
    for k in range(routes_ref.shape[0]):
        table += jnp.where(routes_ref[k : k + 1, :] == ids, gates_ref[k : k + 1, :], 0.0)
    table = table.T
    high = table.astype(jnp.bfloat16)
    out_ref[:, :experts] = high
    out_ref[:, experts:] = (table - high.astype(jnp.float32)).astype(jnp.bfloat16)
    loads[2].wait()


def assign_table(routes, gates, saved, experts):
    vmem, hbm = pl.BlockSpec(memory_space=pltpu.VMEM), pl.BlockSpec(memory_space=pl.ANY)
    return pl.pallas_call(
        table_kernel,
        out_shape=[
            jax.ShapeDtypeStruct((routes.shape[0], 2 * experts), jnp.bfloat16),
            jax.ShapeDtypeStruct(saved.shape, saved.dtype),
        ],
        in_specs=[hbm] * 3,
        out_specs=[vmem] * 2,
        scratch_shapes=[
            pltpu.VMEM(routes.shape[::-1], routes.dtype),
            pltpu.VMEM(gates.shape[::-1], gates.dtype),
            pltpu.SemaphoreType.DMA((3,)),
        ],
        compiler_params=pltpu.CompilerParams(vmem_limit_bytes=MIB),
    )(*[in_space(x, pltpu.HBM) for x in (routes.T, gates.T, saved)])


def join_kernel(count, *refs):
    out_ref = refs[-1]
    at = 0
    for ref in refs[:count]:
        out_ref[:, at : at + ref.shape[1]] = ref[...]
        at += ref.shape[1]


def join(parts, after=()):
    vmem, hbm = pl.BlockSpec(memory_space=pltpu.VMEM), pl.BlockSpec(memory_space=pl.ANY)
    width = sum(part.shape[1] for part in parts)
    return pl.pallas_call(
        functools.partial(join_kernel, len(parts)),
        out_shape=jax.ShapeDtypeStruct((parts[0].shape[0], width), parts[0].dtype),
        in_specs=[vmem] * len(parts) + [hbm] * len(after),
        out_specs=vmem,
        compiler_params=pltpu.CompilerParams(vmem_limit_bytes=4 * MIB),
    )(*parts, *after)


def gather_tokens(grad, table):
    peers = lax.axis_size("expert")
    top = peers // 2
    middle = [1 << b for b in reversed(range(2, top.bit_length() - 1))]
    width = grad.shape[1]
    names, tables = [0], table

    def add_tables(got, delta):
        nonlocal names, tables
        names, tables = names + [k ^ delta for k in names], jnp.concatenate([tables, got], axis=1)

    def with_tables(k, delta, after=()):
        got = exchange(join([chunks[k], tables], after), delta)
        chunks[k ^ delta] = got[:, :width]
        add_tables(got[:, width:], delta)

    near, far = [0], [top]
    for delta in middle:
        near += [k ^ delta for k in near]
    chunks = {k: from_next_section(grad, k) for k in [PAIR] + near[1:] + [top, 0]}
    add_tables(exchange(tables, top), top)
    for delta in middle:
        for k in far[:-1]:
            chunks[k ^ delta] = exchange(chunks[k], delta)
        with_tables(far[-1], delta)
        far += [k ^ delta for k in far]
    rest = far + near[1:]
    for k in rest[:-1]:
        chunks[k ^ PAIR] = exchange(chunks[k], PAIR)
    with_tables(rest[-1], PAIR, after=[chunks[PAIR]])
    late = [near[-1] ^ PAIR, far[-1] ^ PAIR]
    return chunks, late, [(names, tables), ([k ^ CORE for k in names], exchange(tables, CORE))]


def swap_cores(chunks, late, waits):
    early = [k for k in chunks if k not in late]
    groups = []
    for part, after in ((early, ()), (late, waits)):
        own = jnp.concatenate([chunks[k] for k in part])
        if after:
            own = join([own], after=after)
        groups.append([(part, own), ([k ^ CORE for k in part], exchange(own, CORE))])
    return groups


def slot_units(order, most):
    blocks = -(-ROWS // most)
    return blocks, list(dict.fromkeys(delta // blocks for delta in order))


def slot_bases(order, most, tok, me):
    blocks, units = slot_units(order, most)
    part = lax.broadcasted_iota(jnp.int32, (1, len(order) * tok), 1) // tok
    bases = jnp.zeros_like(part)
    for i, delta in enumerate(order):
        base = units.index(delta // blocks) * blocks * most + (me ^ delta) % blocks * most
        bases = jnp.where(part == i, base, bases)
    return bases


def find_slots(order, table_order, tok, most, me, table_refs, table_ref):
    experts = table_ref.shape[1] // 2
    count = len(order) * tok
    for names, ref in zip(table_order, table_refs, strict=True):
        for n, k in enumerate(names):
            i = order.index(k)
            table_ref[i * tok : (i + 1) * tok, :] = ref[:, n * 2 * experts : (n + 1) * 2 * experts]
    lanes = lax.broadcasted_iota(jnp.int32, (8, 2 * experts), 1)
    pick = jnp.where((lanes == me) | (lanes == me + experts), 1.0, 0.0).astype(jnp.bfloat16)
    gate = lax.dot_general(pick, table_ref[...], CONTRACT_LAST, preferred_element_type=jnp.float32)
    live = gate > 0.0
    rows = lax.broadcasted_iota(jnp.int32, (count, count), 0)
    cols = lax.broadcasted_iota(jnp.int32, (count, count), 1)
    earlier = jnp.where((rows < cols) & (rows // tok == cols // tok), 1.0, 0.0).astype(jnp.bfloat16)
    before = lax.dot_general(
        jnp.where(live, 1.0, 0.0).astype(jnp.bfloat16),
        earlier,
        (((1,), (0,)), ((), ())),
        preferred_element_type=jnp.float32,
    )
    slot = jnp.where(live[:1], slot_bases(order, most, tok, me) + before[:1].astype(jnp.int32), -1)
    return slot, gate[:1]


def fill_rows(out_ref, token_ref, slot, gate, first, height, add=False):
    hit = first + lax.broadcasted_iota(jnp.int32, (height, slot.shape[1]), 0) == slot
    weight = jnp.sum(jnp.where(hit, gate, 0.0), axis=1, keepdims=True)
    onehot = jnp.where(hit, 1.0, 0.0).astype(jnp.bfloat16)
    width = token_ref.shape[1]
    step = 512 if width % 512 == 0 else width
    for k in range(0, width, step):
        taken = jnp.dot(onehot, token_ref[:, k : k + step], preferred_element_type=jnp.float32)
        scaled = (weight * taken).astype(out_ref.dtype)
        if add:
            scaled += out_ref[first : first + height, k : k + step]
        out_ref[first : first + height, k : k + step] = scaled


def arrange_kernel(order, table_order, tok, most, *refs):
    me_ref, w_hbm = refs[:2]
    table_refs = refs[2 : 2 + len(table_order)]
    token_refs = refs[2 + len(table_order) : -6]
    rows_ref, slot_ref, gate_ref, w_ref, table_ref, sems = refs[-6:]
    tall = w_ref.shape[0] // W_LOADS
    loads = [
        pltpu.make_async_copy(w_hbm.at[pl.ds(n * tall, tall)], w_ref.at[pl.ds(n * tall, tall)], sems.at[n])
        for n in range(W_LOADS)
    ]
    for load in loads:
        load.start()
    slot, gate = find_slots(order, table_order, tok, most, me_ref[0], table_refs, table_ref)
    slot_ref[...] = slot
    gate_ref[...] = gate
    token, row = 0, 0
    for ref in token_refs:
        count = ref.shape[0]
        height = count // tok * most
        span = slice(token, token + count)
        if most >= ROWS:
            fill_rows(rows_ref, ref, slot[:, span], gate[:, span], row, height)
        else:
            fill_rows(rows_ref, ref, slot[:, span], gate[:, span], 0, rows_ref.shape[0], add=token > 0)
        token, row = token + count, row + height
    for load in loads:
        load.wait()


def down_kernel(order, tok, most, me_ref, slot_ref, gate_ref, saved_ref, first_ref, w_hbm, early_ref, *refs):
    token_refs, (out_hbm, d_ref, w_ref, out_ref, sems, out_sems) = refs[:-6], refs[-6:]
    width = w_ref.shape[0]
    blocks, units = slot_units(order, most)
    tall = blocks * most
    me = me_ref[0]
    wide = width // W_PARTS
    height = wide // W_LOADS

    def load(n):
        part = pl.ds(pl.multiple_of(n * height, height), height)
        return pltpu.make_async_copy(w_hbm.at[part], w_ref.at[part], sems.at[n])

    def stores(part):
        for half in range(2):
            span = pl.ds(pl.multiple_of(half * width + part * wide, wide), wide)
            yield pltpu.make_async_copy(out_ref.at[:, span], out_hbm.at[:, span], out_sems.at[2 * part + half])

    for n in range(W_LOADS, W_PARTS * W_LOADS):
        load(n).start()
    for n in range(W_LOADS):
        part = pl.ds(n * height, height)
        pltpu.make_async_copy(first_ref.at[part], w_ref.at[part], sems.at[n]).start()
    row = early_ref.shape[0]
    d_ref[:row, :] = early_ref[...]
    token = len(order) * tok - sum(ref.shape[0] for ref in token_refs)
    for ref in token_refs:
        count = ref.shape[0]
        size = count // tok * most
        span = slice(token, token + count)
        if blocks == 1:
            fill_rows(d_ref, ref, slot_ref[:, span], gate_ref[:, span], row, size)
        else:
            fill_rows(d_ref, ref, slot_ref[:, span], gate_ref[:, span], 0, d_ref.shape[0], add=True)
        token, row = token + count, row + size

    @pl.loop(0, W_PARTS)
    def _(part):
        for n in range(W_LOADS):
            load(part * W_LOADS + n).wait()
        at = pl.multiple_of(part * wide, wide)
        hidden = lax.dot_general(
            d_ref[...], w_ref[pl.ds(at, wide), :], CONTRACT_LAST, preferred_element_type=jnp.float32
        )
        for i, delta in enumerate(units):
            place = pl.ds(pl.multiple_of((me // blocks ^ delta) * tall, tall), tall)
            h = hidden[i * tall : (i + 1) * tall]
            a = saved_ref[place, pl.ds(at, wide)].astype(jnp.float32)
            u = saved_ref[place, pl.ds(width + at, wide)].astype(jnp.float32)
            sig = jax.nn.sigmoid(a)
            hs = h * sig
            out_ref[place, pl.ds(at, wide)] = (hs * u * (1.0 + a * (1.0 - sig))).astype(out_ref.dtype)
            out_ref[place, pl.ds(width + at, wide)] = (hs * a).astype(out_ref.dtype)
        for store in stores(part):
            store.start()

    for part in range(W_PARTS):
        for store in stores(part):
            store.wait()


def per_device(next_grad, routes, gates, saved, w_down):
    experts = lax.axis_size("expert")
    slots, width = saved.shape[2:]
    most = slots // experts
    tok, features = next_grad.shape[1:]
    table, near_saved = assign_table(routes[0], gates[0], saved[0, 0], experts)
    chunks, late, tables = gather_tokens(next_grad[0], table)
    pairs = swap_cores(chunks, late, [array for _, array in tables[1:]])
    (early_own, early_other), (late_own, late_other) = pairs
    order = [k for names, _ in (early_own, early_other, late_own, late_other) for k in names]
    me = lax.axis_index("expert").astype(jnp.int32).reshape(1)
    smem = pl.BlockSpec(memory_space=pltpu.SMEM)
    vmem, hbm = pl.BlockSpec(memory_space=pltpu.VMEM), pl.BlockSpec(memory_space=pl.ANY)
    count = experts * tok
    early = early_own[1].shape[0] * 2 // tok * most if most >= ROWS else slots
    rows, slot, gate, first = pl.pallas_call(
        functools.partial(arrange_kernel, order, [names for names, _ in tables], tok, most),
        out_shape=[
            jax.ShapeDtypeStruct((early, features), jnp.bfloat16),
            jax.ShapeDtypeStruct((1, count), jnp.int32),
            jax.ShapeDtypeStruct((1, count), jnp.float32),
            jax.ShapeDtypeStruct((width // 2 // W_PARTS, features), w_down.dtype),
        ],
        in_specs=[smem, hbm] + [vmem] * (len(tables) + 2),
        out_specs=[vmem] * 4,
        scratch_shapes=[
            pltpu.VMEM((count, 2 * experts), jnp.bfloat16),
            pltpu.SemaphoreType.DMA((W_LOADS,)),
        ],
        compiler_params=pltpu.CompilerParams(vmem_limit_bytes=16 * MIB),
    )(
        me,
        in_space(w_down[0], pltpu.HBM),
        *[array for _, array in tables],
        early_own[1],
        early_other[1],
    )
    out = pl.pallas_call(
        functools.partial(down_kernel, order, tok, most),
        out_shape=jax.ShapeDtypeStruct((slots, width), jnp.bfloat16),
        in_specs=[smem, vmem, vmem, vmem, vmem, hbm, vmem, vmem, vmem],
        out_specs=hbm,
        scratch_shapes=[
            pltpu.VMEM((slots, features), jnp.bfloat16),
            pltpu.VMEM(w_down.shape[1:], jnp.bfloat16),
            pltpu.VMEM((slots, width), jnp.bfloat16),
            pltpu.SemaphoreType.DMA((W_PARTS * W_LOADS,)),
            pltpu.SemaphoreType.DMA((2 * W_PARTS,)),
        ],
        compiler_params=pltpu.CompilerParams(vmem_limit_bytes=40 * MIB),
    )(
        me,
        slot,
        gate,
        near_saved,
        first,
        in_space(w_down[0], pltpu.HBM),
        rows,
        late_own[1],
        late_other[1],
    )
    return out[None, None]


def solution(mesh):
    return jax.shard_map(
        per_device,
        mesh=mesh,
        in_specs=(
            P("section", "expert", None),
            P("section", "expert", None),
            P("section", "expert", None),
            P("section", "expert", None, None),
            P("expert", None, None),
        ),
        out_specs=P("section", "expert", None, None),
        check_vma=False,
    )
```
